32 devices in a mesh: req: 8 (over z, x), mlp: 4 (over y, core).
Axes of the slice: x: 2, y: 2, z: 4, core: 2. Of those that a mesh axis runs over, the one named last changes fastest.
Arguments:
- patches: bfloat16 [2048, 4, 1664], P('req', 'mlp'), may hold values from -6 to 6
- vis_gain: float32 [1664], replicated, may hold values from 0.1 to 1.9
- vis_proj: bfloat16 [6656, 1664], P('mlp'), may hold values from -0.078125 to 0.078125
- targets: int32 [2048], P('req'), may hold values from 0 to 8191, as said below
- lengths: int32 [8], P('req'), may hold values from 512 to 1024, as said below
- text: bfloat16 [8192, 1664], P('req'), may hold values from -6 to 6
- attn_gain: float32 [1664], replicated, may hold values from 0.1 to 1.9
- wqkv: bfloat16 [1664, 4992], P(None, 'mlp'), as said below
- wo: bfloat16 [1664, 1664], P('mlp'), may hold values from -0.15625 to 0.15625
- mlp_gain: float32 [1664], replicated, may hold values from 0.1 to 1.9
- w_in: bfloat16 [1664, 8192], P('req', 'mlp'), may hold values from -0.15625 to 0.15625
- w_out: bfloat16 [8192, 1664], P('mlp', 'req'), may hold values from -0.0625 to 0.0625
Outputs:
- layer_out: bfloat16 [8192, 1664], P(('req', 'mlp'))
The draws below stay inside these ranges and needn't reach their ends.
Inputs may be any that keep to these rules, and one draw needn't show every extreme that they name: targets[m] = 1024 * prompt + slot, all distinct, every slot below its prompt's length. The rows of one vision device go to one prompt 64 times at most, and this is reached in every draw. `lengths`: some prompt has length 1024. `wqkv`: projection weights, each within -1.8 to 1.8; a head's query and key columns may be much larger than its value columns.
All inputs are finite; a program needn't handle non-finite values.
Results may differ from the reference program's by a relative error of at most 0.027.
The reference program's roundings to bfloat16 on the way count: a program that leaves them out, or rounds other values in their place, can miss the bound.
Values may be sent and summed in bfloat16 or wider, within the bound.
A program may use at most 128 MiB of HBM per device.

```python
import jax
import jax.numpy as jnp
from jax import lax

D = 1664
HEADS = 16
HD = 104
FF = 8192
SEQ = 1024
MERGED = 256
REQS = 8
CAP = 64
SLOTS = 2048
N_MLP = 4


def shared_plan(key):
    base = jax.random.fold_in(key, 11)
    key_len, key_forced, key_lift, key_perm, key_order, key_shuffle = jax.random.split(base, 6)
    prompt_ids = jnp.arange(REQS)
    prompt_len = jax.random.randint(key_len, (REQS,), 2 * MERGED, SEQ + 1)
    forced = jax.random.randint(key_forced, (), 0, REQS)
    prompt_len = jnp.where(prompt_ids == forced, SEQ, prompt_len).astype(jnp.int32)
    half_cap = CAP // 2
    lifted = jax.random.randint(key_lift, (REQS, REQS // 2), 0, half_cap + 1)
    lifted = lifted.at[:, 0].set(half_cap)
    loads = jnp.stack([half_cap + lifted, half_cap - lifted], axis=-1).reshape(REQS, REQS)
    orders_dest = jax.vmap(lambda sub_key: jax.random.permutation(sub_key, REQS))(jax.random.split(key_perm, REQS))
    counts = jnp.zeros((REQS, REQS), jnp.int32).at[prompt_ids[:, None], orders_dest].set(loads.astype(jnp.int32))
    earlier = jnp.cumsum(counts, axis=0) - counts
    slot_orders = jax.vmap(lambda sub_key: jax.random.permutation(sub_key, SEQ))(jax.random.split(key_order, REQS))
    outside = (slot_orders >= prompt_len[:, None]).astype(jnp.int32)
    ranking = jnp.argsort(outside, axis=1, stable=True)
    free_slots = jnp.take_along_axis(slot_orders, ranking, axis=1)

    def one_source(counts_row, offsets, sub_key):
        ends = jnp.cumsum(counts_row)
        slot_ids = jnp.arange(MERGED)
        target_req = jnp.sum((ends[None, :] <= slot_ids[:, None]).astype(jnp.int32), axis=1)
        inner = slot_ids - (ends[target_req] - counts_row[target_req])
        position = free_slots[target_req, offsets[target_req] + inner]
        flat_index = target_req * SEQ + position
        return flat_index[jax.random.permutation(sub_key, MERGED)]
    flat_all = jax.vmap(one_source)(counts, earlier, jax.random.split(key_shuffle, REQS))
    return (flat_all.reshape(-1).astype(jnp.int32), prompt_len)


def draw_targets(key, part):
    return shared_plan(key)[0]


def draw_lengths(key, part):
    return shared_plan(key)[1]


def draw_wqkv(key, part):
    values = jax.random.normal(key, (D, HEADS * 3 * HD), jnp.float32)
    values = jnp.clip(values, -6.0, 6.0) / jnp.float32(D) ** 0.5
    return values.astype(jnp.bfloat16)


def levels(stream_key, extent, pieces, low, top_value):
    level, own = 1.0, jax.random.fold_in(stream_key, 6)
    for axis_at, blocks in pieces:
        heights = jnp.exp(jax.random.uniform(jax.random.fold_in(own, axis_at), (blocks,), jnp.float32, low / len(pieces), top_value / len(pieces)))
        level = level * jnp.repeat(heights, extent[axis_at] // blocks).reshape([-1 if axis == axis_at else 1 for axis in range(len(extent))])
    return level


def bell_draw(stream_key, shape, deviation, limit, pieces=(), dtype=jnp.bfloat16):
    loudness = levels(stream_key, shape, pieces, -0.22, 0.18) if pieces else 1.0
    array = jax.random.normal(stream_key, shape, jnp.float32) * deviation * loudness
    return jnp.minimum(jnp.maximum(array, -limit), limit).astype(dtype)


def setup_inputs(seed: int = 0) -> dict:
    streams_of = jax.random.split(jax.random.key(seed), 13)
    return {
        "patches": bell_draw(streams_of[0], (SLOTS, 4, D), 1.0, 6.0, ((0, 8), (1, 4))),
        "vis_gain": jnp.clip(1.0 + 0.18 * jax.random.normal(streams_of[1], (D,), jnp.float32), 0.1, 1.9),
        "vis_proj": bell_draw(streams_of[2], (4 * D, D), (4 * D) ** -0.5, 0.078125, ((0, 4),)),
        "targets": draw_targets(jax.random.fold_in(streams_of[12], 71), 0),
        "lengths": draw_lengths(jax.random.fold_in(streams_of[12], 71), 0),
        "text": bell_draw(streams_of[5], (REQS * SEQ, D), 1.0, 6.0, ((0, 8),)),
        "attn_gain": jnp.clip(1.0 + 0.18 * jax.random.normal(streams_of[6], (D,), jnp.float32), 0.1, 1.9),
        "wqkv": draw_wqkv(jax.random.fold_in(streams_of[12], 71), 0),
        "wo": bell_draw(streams_of[8], (HEADS * HD, D), (HEADS * HD) ** -0.5, 0.15625, ((0, 4),)),
        "mlp_gain": jnp.clip(1.0 + 0.18 * jax.random.normal(streams_of[9], (D,), jnp.float32), 0.1, 1.9),
        "w_in": bell_draw(streams_of[10], (D, FF), D ** -0.5, 0.15625, ((0, 8), (1, 4))),
        "w_out": bell_draw(streams_of[11], (FF, D), FF ** -0.5, 0.0625, ((0, 4), (1, 8))),
    }


def rms_scale(values, gain):
    wide = values.astype(jnp.float32)
    power = lax.optimization_barrier(jnp.mean(wide * wide, axis=-1, keepdims=True))
    return wide * lax.rsqrt(power + 1e-06) * gain

def per_prompt(item, wqkv, wo, attn_gain, mlp_gain, w_in, w_out):
    embedded, length = item
    attn_in = rms_scale(embedded, attn_gain).astype(jnp.bfloat16)
    qkv = jnp.dot(attn_in, wqkv, preferred_element_type=jnp.float32).astype(jnp.bfloat16)
    qkv = qkv.reshape(SEQ, HEADS, 3, HD).astype(jnp.float32)
    query, keys, values = (qkv[:, :, 0], qkv[:, :, 1], qkv[:, :, 2])
    scores = jnp.einsum('qhd,khd->hqk', query, keys) / jnp.float32(HD) ** 0.5
    row_ids = jnp.arange(SEQ)
    causal = row_ids[None, :] <= row_ids[:, None]
    scores = jnp.where(causal[None], scores, jnp.float32(-1e+30))
    peak = lax.optimization_barrier(jnp.max(scores, axis=-1, keepdims=True))
    weights = jnp.exp(scores - peak)
    probs = (weights / lax.optimization_barrier(jnp.sum(weights, axis=-1, keepdims=True))).astype(jnp.bfloat16)
    context = jnp.einsum('hqk,khd->qhd', probs.astype(jnp.float32), values).astype(jnp.bfloat16)
    context = context.reshape(SEQ, HEADS * HD)
    group_cols = HEADS * HD // N_MLP
    attn_total = jnp.zeros((SEQ, D), jnp.float32)
    for group in range(N_MLP):
        piece = jnp.dot(context[:, group * group_cols:(group + 1) * group_cols], wo[group * group_cols:(group + 1) * group_cols], preferred_element_type=jnp.float32)
        attn_total = attn_total + lax.optimization_barrier(piece.astype(jnp.bfloat16)).astype(jnp.float32)
    resid = embedded.astype(jnp.float32) + attn_total
    mlp_in = rms_scale(resid, mlp_gain).astype(jnp.bfloat16)
    hidden_cols = FF // N_MLP
    mlp_total = jnp.zeros((SEQ, D), jnp.float32)
    for group in range(N_MLP):
        upward = jnp.dot(mlp_in, w_in[:, group * hidden_cols:(group + 1) * hidden_cols], preferred_element_type=jnp.float32)
        active = jax.nn.gelu(upward, approximate=False).astype(jnp.bfloat16)
        piece = jnp.dot(active, w_out[group * hidden_cols:(group + 1) * hidden_cols], preferred_element_type=jnp.float32)
        mlp_total = mlp_total + lax.optimization_barrier(piece.astype(jnp.bfloat16)).astype(jnp.float32)
    result = resid + mlp_total
    valid = row_ids < length
    return jnp.where(valid[:, None], result, jnp.float32(0.0)).astype(jnp.bfloat16)

def reference(patches, vis_gain, vis_proj, targets, lengths, text, attn_gain, wqkv, wo, mlp_gain, w_in, w_out):
    patch_norm = rms_scale(patches, vis_gain).astype(jnp.bfloat16)
    merged_rows = patch_norm.reshape(patches.shape[0], 4 * D)
    image_rows = jnp.dot(merged_rows, vis_proj, preferred_element_type=jnp.float32).astype(jnp.bfloat16)
    embedded = text.at[targets].set(image_rows)
    prompts = embedded.reshape(REQS, SEQ, D)

    def apply_one(item):
        return per_prompt(item, wqkv, wo, attn_gain, mlp_gain, w_in, w_out)
    result = lax.map(apply_one, (prompts, lengths))
    return result.reshape(REQS * SEQ, D)
```

```python
import jax
import jax.numpy as jnp
from jax import lax
from jax.sharding import PartitionSpec as P

HD = 104
CHUNKS = 2
PHASES = 4


def rms_scale(values, gain):
    wide = values.astype(jnp.float32)
    power = jnp.mean(wide * wide, axis=-1, keepdims=True)
    return wide * lax.rsqrt(power + 1e-06) * gain


def shards(
    patches, vis_gain, vis_proj, targets, lengths, text, attn_gain, wqkv, wo, mlp_gain, w_in, w_out
):
    requests = lax.axis_size("req")
    groups = lax.axis_size("mlp")
    seq_len, width = text.shape
    merged_count = patches.shape[0]
    capacity = 2 * merged_count // requests
    steps = requests // 2
    flip = [(i, i ^ 1) for i in range(requests)]
    onward = [(i, (i + 2) % requests) for i in range(requests)]
    chain = {"hand": (w_in, w_out.T), "pairs": [], "step": 0}

    def advance(phase, tied):
        new = []
        while chain["step"] < (phase + 1) * steps // PHASES:
            hand = chain["hand"]
            across = tuple(lax.ppermute(block, "req", flip) for block in hand)
            chain["pairs"].append([hand, across])
            chain["step"] += 1
            if chain["step"] < steps:
                chain["hand"] = tuple(lax.ppermute(block, "req", onward) for block in hand)
            new.append(len(chain["pairs"]) - 1)
        if tied is None:
            return None
        across = [chain["pairs"][i][1] for i in new]
        tied, across, chain["hand"] = lax.optimization_barrier((tied, across, chain["hand"]))
        for i, value in zip(new, across):
            chain["pairs"][i][1] = value
        return tied

    def gathered(which):
        me = lax.axis_index("req")
        full = jnp.zeros((requests, *chain["pairs"][0][0][which].shape), jnp.bfloat16)
        for step, (own, across) in enumerate(chain["pairs"]):
            source = (me - 2 * step) % requests
            full = lax.dynamic_update_index_in_dim(full, own[which], source, 0)
            full = lax.dynamic_update_index_in_dim(full, across[which], source ^ 1, 0)
        return full.reshape(-1, full.shape[-1])

    patch_norm = rms_scale(patches[:, 0, :], vis_gain).astype(jnp.bfloat16)
    partial_value = jnp.dot(patch_norm, vis_proj, preferred_element_type=jnp.float32)
    image_rows = lax.psum(partial_value.astype(jnp.bfloat16), "mlp")
    image_rows = advance(0, image_rows)
    target_req = targets // seq_len
    position = targets % seq_len
    order = jnp.arange(merged_count)
    same = (target_req[:, None] == target_req[None, :]) & (order[None, :] < order[:, None])
    rank_in = jnp.sum(same.astype(jnp.int32), axis=1)
    slot_ids = target_req * capacity + rank_in
    pick = slot_ids[None, :] == jnp.arange(requests * capacity)[:, None]
    slot_fill = jnp.max(jnp.where(pick, position[None, :], -1), axis=1).reshape(requests, capacity)
    got_slots = lax.all_to_all(slot_fill, "req", split_axis=0, concat_axis=0, tiled=True)
    buffer = jnp.dot(
        pick.astype(jnp.bfloat16), image_rows, preferred_element_type=jnp.float32
    ).astype(jnp.bfloat16)
    received = lax.all_to_all(
        buffer.reshape(requests, capacity, width), "req", split_axis=0, concat_axis=0, tiled=True
    )
    received = advance(1, received)
    arrived = received.reshape(requests * capacity, width)
    place = got_slots.reshape(-1)[None, :] == jnp.arange(seq_len)[:, None]
    placed = jnp.dot(place.astype(jnp.bfloat16), arrived, preferred_element_type=jnp.float32)
    hit = jnp.any(place, axis=1, keepdims=True)
    embedded = jnp.where(hit, placed.astype(jnp.bfloat16), text)

    attn_in = rms_scale(embedded, attn_gain).astype(jnp.bfloat16)
    qkv = jnp.dot(attn_in, wqkv, preferred_element_type=jnp.float32).astype(jnp.bfloat16)
    qkv = advance(2, qkv)
    advance(3, None)
    local_heads = wqkv.shape[1] // (3 * HD)
    qkv = qkv.reshape(seq_len, local_heads, 3, HD)
    query, keys, values = (qkv[:, :, 0], qkv[:, :, 1], qkv[:, :, 2])
    share_rows = seq_len // groups
    piece = share_rows // CHUNKS

    def chunk_of(array, j):
        cut = array.reshape(groups, CHUNKS, piece, *array.shape[1:])[:, j]
        return cut.reshape(groups * piece, *array.shape[1:])

    row_ids = jnp.arange(seq_len)
    sums = []
    for j in range(CHUNKS):
        rows = chunk_of(row_ids, j)
        scores = (
            jnp.einsum("qhd,khd->hqk", chunk_of(query, j), keys, preferred_element_type=jnp.float32)
            / jnp.float32(HD) ** 0.5
        )
        causal = row_ids[None, :] <= rows[:, None]
        scores = jnp.where(causal[None], scores, jnp.float32(-1e30))
        peak = jnp.max(scores, axis=-1, keepdims=True)
        weights = jnp.exp(scores - peak)
        probs = (weights / jnp.sum(weights, axis=-1, keepdims=True)).astype(jnp.bfloat16)
        context = jnp.einsum(
            "hqk,khd->qhd", probs, values, preferred_element_type=jnp.float32
        ).astype(jnp.bfloat16)
        context = context.reshape(groups * piece, local_heads * HD)
        attn_part = jnp.dot(context, wo, preferred_element_type=jnp.float32)
        sums.append(
            lax.psum_scatter(
                attn_part.astype(jnp.bfloat16), "mlp", scatter_dimension=0, tiled=True
            )
        )
    group = lax.axis_index("mlp")
    own_embedded = lax.dynamic_slice_in_dim(embedded, group * share_rows, share_rows, 0)
    resids, inputs = [], []
    for j in range(CHUNKS):
        own = own_embedded[j * piece : (j + 1) * piece]
        resid = own.astype(jnp.float32) + sums[j].astype(jnp.float32)
        resids.append(resid)
        mlp_in = rms_scale(resid, mlp_gain).astype(jnp.bfloat16)
        inputs.append(lax.all_gather(mlp_in, "mlp", axis=0, tiled=True))
    w_in_full, w_out_full = gathered(0), gathered(1)
    outs = []
    for j in range(CHUNKS):
        mlp_in = inputs[j]
        upward = jnp.dot(mlp_in, w_in_full, preferred_element_type=jnp.float32)
        active = jax.nn.gelu(upward, approximate=False).astype(jnp.bfloat16)
        mlp_part = lax.dot_general(
            active, w_out_full, (((1,), (1,)), ((), ())), preferred_element_type=jnp.float32
        )
        mlp_share = lax.psum_scatter(
            mlp_part.astype(jnp.bfloat16), "mlp", scatter_dimension=0, tiled=True
        ).astype(jnp.float32)
        result = resids[j] + mlp_share
        ids = group * share_rows + j * piece + jnp.arange(piece)
        outs.append(jnp.where((ids < lengths[0])[:, None], result, 0.0).astype(jnp.bfloat16))
    return jnp.concatenate(outs, axis=0)


def solution(mesh):
    return jax.shard_map(
        shards,
        mesh=mesh,
        in_specs=(
            P("req", "mlp", None),
            P(),
            P("mlp", None),
            P("req"),
            P("req"),
            P("req", None),
            P(),
            P(None, "mlp"),
            P("mlp", None),
            P(),
            P("req", "mlp"),
            P("mlp", "req"),
        ),
        out_specs=P(("req", "mlp"), None),
        check_vma=False,
    )
```

```python
import jax
import jax.numpy as jnp
from jax import lax
from jax.sharding import PartitionSpec as P

HD = 104
CHUNKS = 2
PHASES = 4


def rms_scale(values, gain):
    wide = values.astype(jnp.float32)
    power = jnp.mean(wide * wide, axis=-1, keepdims=True)
    return wide * lax.rsqrt(power + 1e-06) * gain


def shards(
    patches, vis_gain, vis_proj, targets, lengths, text, attn_gain, wqkv, wo, mlp_gain, w_in, w_out
):
    requests = lax.axis_size("req")
    groups = lax.axis_size("mlp")
    seq_len, width = text.shape
    merged_count = patches.shape[0]
    capacity = 2 * merged_count // requests
    steps = requests // 2
    flip = [(i, i ^ 1) for i in range(requests)]
    onward = [(i, (i + 2) % requests) for i in range(requests)]
    chain = {"hand": (w_in, w_out.T), "pairs": [], "step": 0}

    def advance(phase, tied):
        new = []
        while chain["step"] < (phase + 1) * steps // PHASES:
            hand = chain["hand"]
            across = tuple(lax.ppermute(block, "req", flip) for block in hand)
            chain["pairs"].append([hand, across])
            chain["step"] += 1
            if chain["step"] < steps:
                chain["hand"] = tuple(lax.ppermute(block, "req", onward) for block in hand)
            new.append(len(chain["pairs"]) - 1)
        if tied is None:
            return None
        across = [chain["pairs"][i][1] for i in new]
        tied, across, chain["hand"] = lax.optimization_barrier((tied, across, chain["hand"]))
        for i, value in zip(new, across):
            chain["pairs"][i][1] = value
        return tied

    def gathered(which):
        return jnp.concatenate([part[which] for pair in chain["pairs"] for part in pair], axis=0)

    me = lax.axis_index("req")
    group = lax.axis_index("mlp")
    shard = width // requests
    at = jnp.arange(width) // shard
    source = ((me - 2 * (at // 2)) % requests) ^ (at % 2)
    feature = source * shard + jnp.arange(width) % shard
    column_map = (feature[None, :] == jnp.arange(width)[:, None]).astype(jnp.bfloat16)

    def swap(value, bit):
        return lax.ppermute(value, "mlp", [(i, i ^ bit) for i in range(groups)])

    def narrow_sum(first, second):
        return (first.astype(jnp.float32) + second.astype(jnp.float32)).astype(jnp.bfloat16)

    def reduce_share(parts):
        blocks = parts.reshape(2, 2, -1, parts.shape[-1])
        held = narrow_sum(blocks[:, 0], swap(blocks[:, 1], 1))
        return held[0], swap(held[1], 2)

    def gather_shares(share):
        half = jnp.stack([share, swap(share, 2)])
        return jnp.stack([half, swap(half, 1)], axis=1).reshape(-1, share.shape[-1])

    patch_norm = rms_scale(patches[:, 0, :], vis_gain).astype(jnp.bfloat16)
    partial_value = jnp.dot(patch_norm, vis_proj, preferred_element_type=jnp.float32)
    halves = partial_value.astype(jnp.bfloat16).reshape(2, merged_count // 2, width)
    core = group % 2
    mine = lax.dynamic_index_in_dim(halves, core, 0, keepdims=False)
    other = lax.dynamic_index_in_dim(halves, 1 - core, 0, keepdims=False)
    held = narrow_sum(mine, swap(other, 1))
    held = narrow_sum(held, swap(held, 2))
    across_half = swap(held, 1)
    image_rows = jnp.concatenate(
        [jnp.where(core == 0, held, across_half), jnp.where(core == 0, across_half, held)], axis=0
    )
    image_rows = advance(0, image_rows)
    target_req = targets // seq_len
    position = targets % seq_len
    order = jnp.arange(merged_count)
    same = (target_req[:, None] == target_req[None, :]) & (order[None, :] < order[:, None])
    rank_in = jnp.sum(same.astype(jnp.int32), axis=1)
    slot_ids = target_req * capacity + rank_in
    pick = slot_ids[None, :] == jnp.arange(requests * capacity)[:, None]
    slot_fill = jnp.max(jnp.where(pick, position[None, :], -1), axis=1).reshape(requests, capacity)
    got_slots = lax.all_to_all(slot_fill, "req", split_axis=0, concat_axis=0, tiled=True)
    buffer = jnp.dot(
        pick.astype(jnp.bfloat16), image_rows, preferred_element_type=jnp.float32
    ).astype(jnp.bfloat16)
    received = lax.all_to_all(
        buffer.reshape(requests, capacity, width), "req", split_axis=0, concat_axis=0, tiled=True
    )
    arrived = received.reshape(requests * capacity, width)
    place = got_slots.reshape(-1)[None, :] == jnp.arange(seq_len)[:, None]
    placed = jnp.dot(place.astype(jnp.bfloat16), arrived, preferred_element_type=jnp.float32)
    hit = jnp.any(place, axis=1, keepdims=True)
    embedded = jnp.where(hit, placed.astype(jnp.bfloat16), text)

    attn_in = rms_scale(embedded, attn_gain).astype(jnp.bfloat16)
    qkv = jnp.dot(attn_in, wqkv, preferred_element_type=jnp.float32).astype(jnp.bfloat16)
    qkv = advance(1, qkv)
    local_heads = wqkv.shape[1] // (3 * HD)
    qkv = qkv.reshape(seq_len, local_heads, 3, HD)
    query, keys, values = (qkv[:, :, 0], qkv[:, :, 1], qkv[:, :, 2])
    share_rows = seq_len // groups
    piece = share_rows // CHUNKS

    def chunk_of(array, j):
        cut = array.reshape(groups, CHUNKS, piece, *array.shape[1:])[:, j]
        return cut.reshape(groups * piece, *array.shape[1:])

    row_ids = jnp.arange(seq_len)
    block_ids = group ^ jnp.arange(groups)
    query_rows = (block_ids[:, None] * share_rows + jnp.arange(share_rows)).reshape(-1)
    query_blocks = query.reshape(groups, share_rows, local_heads, HD)
    query = jnp.concatenate(
        [
            lax.dynamic_index_in_dim(query_blocks, group ^ r, 0, keepdims=False)
            for r in range(groups)
        ],
        axis=0,
    )
    sums = []
    for j in range(CHUNKS):
        rows = chunk_of(query_rows, j)
        scores = (
            jnp.einsum("qhd,khd->hqk", chunk_of(query, j), keys, preferred_element_type=jnp.float32)
            / jnp.float32(HD) ** 0.5
        )
        causal = row_ids[None, :] <= rows[:, None]
        scores = jnp.where(causal[None], scores, jnp.float32(-1e30))
        peak = jnp.max(scores, axis=-1, keepdims=True)
        weights = jnp.exp(scores - peak)
        probs = (weights / jnp.sum(weights, axis=-1, keepdims=True)).astype(jnp.bfloat16)
        context = jnp.einsum(
            "hqk,khd->qhd", probs, values, preferred_element_type=jnp.float32
        ).astype(jnp.bfloat16)
        context = context.reshape(groups * piece, local_heads * HD)
        attn_part = jnp.dot(context, wo, preferred_element_type=jnp.float32)
        attn_part = attn_part.astype(jnp.bfloat16)
        if j == CHUNKS - 1:
            attn_part = advance(2, attn_part)
        sums.append(reduce_share(attn_part))
    advance(3, None)
    own_embedded = lax.dynamic_slice_in_dim(embedded, group * share_rows, share_rows, 0)
    resids, inputs = [], []
    for j in range(CHUNKS):
        own = own_embedded[j * piece : (j + 1) * piece]
        resid = own.astype(jnp.float32) + narrow_sum(*sums[j]).astype(jnp.float32)
        resids.append(resid)
        mlp_in = rms_scale(resid, mlp_gain).astype(jnp.bfloat16)
        mlp_in = jnp.dot(mlp_in, column_map, preferred_element_type=jnp.float32)
        inputs.append(gather_shares(mlp_in.astype(jnp.bfloat16)))
    w_in_full, w_out_full = gathered(0), gathered(1)
    outs = []
    for j in range(CHUNKS):
        mlp_in = inputs[j]
        upward = jnp.dot(mlp_in, w_in_full, preferred_element_type=jnp.float32)
        active = jax.nn.gelu(upward, approximate=False).astype(jnp.bfloat16)
        mlp_part = lax.dot_general(
            active, w_out_full, (((1,), (1,)), ((), ())), preferred_element_type=jnp.float32
        )
        terms = jnp.concatenate(reduce_share(mlp_part.astype(jnp.bfloat16)), axis=0)
        terms = lax.dot_general(
            terms, column_map, (((1,), (1,)), ((), ())), preferred_element_type=jnp.float32
        )
        mlp_share = terms[:piece] + terms[piece:]
        result = resids[j] + mlp_share
        ids = group * share_rows + j * piece + jnp.arange(piece)
        outs.append(jnp.where((ids < lengths[0])[:, None], result, 0.0).astype(jnp.bfloat16))
    return jnp.concatenate(outs, axis=0)


def solution(mesh):
    return jax.shard_map(
        shards,
        mesh=mesh,
        in_specs=(
            P("req", "mlp", None),
            P(),
            P("mlp", None),
            P("req"),
            P("req"),
            P("req", None),
            P(),
            P(None, "mlp"),
            P("mlp", None),
            P(),
            P("req", "mlp"),
            P("mlp", "req"),
        ),
        out_specs=P(("req", "mlp"), None),
        check_vma=False,
    )
```

```python
import jax
import jax.numpy as jnp
from jax import lax
from jax.sharding import PartitionSpec as P

HD = 104
CHUNKS = 2
PHASES = 4


def rms_scale(values, gain):
    wide = values.astype(jnp.float32)
    power = jnp.mean(wide * wide, axis=-1, keepdims=True)
    return wide * lax.rsqrt(power + 1e-06) * gain


def shards(
    patches, vis_gain, vis_proj, targets, lengths, text, attn_gain, wqkv, wo, mlp_gain, w_in, w_out
):
    requests = lax.axis_size("req")
    groups = lax.axis_size("mlp")
    seq_len, width = text.shape
    merged_count = patches.shape[0]
    capacity = 2 * merged_count // requests
    steps = requests // 2
    flip = [(i, i ^ 1) for i in range(requests)]
    onward = [(i, (i + 2) % requests) for i in range(requests)]
    chain = {"hand": (w_in, w_out.T), "pairs": [], "step": 0}

    def advance(phase, tied):
        new = []
        while chain["step"] < (phase + 1) * steps // PHASES:
            hand = chain["hand"]
            across = tuple(lax.ppermute(block, "req", flip) for block in hand)
            chain["pairs"].append([hand, across])
            chain["step"] += 1
            if chain["step"] < steps:
                chain["hand"] = tuple(lax.ppermute(block, "req", onward) for block in hand)
            new.append(len(chain["pairs"]) - 1)
        if tied is None:
            return None
        across = [chain["pairs"][i][1] for i in new]
        tied, across, chain["hand"] = lax.optimization_barrier((tied, across, chain["hand"]))
        for i, value in zip(new, across):
            chain["pairs"][i][1] = value
        return tied

    def gathered(which):
        return jnp.concatenate([part[which] for pair in chain["pairs"] for part in pair], axis=0)

    me = lax.axis_index("req")
    group = lax.axis_index("mlp")
    shard = width // requests
    at = jnp.arange(width) // shard
    source = ((me - 2 * (at // 2)) % requests) ^ (at % 2)
    feature = source * shard + jnp.arange(width) % shard
    column_map = (feature[None, :] == jnp.arange(width)[:, None]).astype(jnp.bfloat16)

    def swap(value, bit):
        return lax.ppermute(value, "mlp", [(i, i ^ bit) for i in range(groups)])

    def narrow_sum(first, second):
        return (first.astype(jnp.float32) + second.astype(jnp.float32)).astype(jnp.bfloat16)

    def reduce_share(parts):
        blocks = parts.reshape(2, 2, -1, parts.shape[-1])
        held = narrow_sum(blocks[:, 0], swap(blocks[:, 1], 1))
        return held[0], swap(held[1], 2)

    def gather_shares(share):
        half = jnp.stack([share, swap(share, 2)])
        return jnp.stack([half, swap(half, 1)], axis=1).reshape(-1, share.shape[-1])

    patch_norm = rms_scale(patches[:, 0, :], vis_gain).astype(jnp.bfloat16)
    partial_value = jnp.dot(patch_norm, vis_proj, preferred_element_type=jnp.float32)
    halves = partial_value.astype(jnp.bfloat16).reshape(2, merged_count // 2, width)
    core = group % 2
    mine = lax.dynamic_index_in_dim(halves, core, 0, keepdims=False)
    other = lax.dynamic_index_in_dim(halves, 1 - core, 0, keepdims=False)
    held = narrow_sum(mine, swap(other, 1))
    held = narrow_sum(held, swap(held, 2))
    across_half = swap(held, 1)
    image_rows = jnp.concatenate(
        [jnp.where(core == 0, held, across_half), jnp.where(core == 0, across_half, held)], axis=0
    )
    target_req = targets // seq_len
    position = targets % seq_len
    order = jnp.arange(merged_count)
    same = (target_req[:, None] == target_req[None, :]) & (order[None, :] < order[:, None])
    rank_in = jnp.sum(same.astype(jnp.int32), axis=1)
    slot_ids = target_req * capacity + rank_in
    pick = slot_ids[None, :] == jnp.arange(requests * capacity)[:, None]
    slot_fill = jnp.max(jnp.where(pick, position[None, :], -1), axis=1).reshape(requests, capacity)
    got_slots = lax.all_to_all(slot_fill, "req", split_axis=0, concat_axis=0, tiled=True)
    quarter = capacity // groups
    own_ids = jnp.arange(requests)[:, None] * capacity + group * quarter + jnp.arange(quarter)
    pick_own = (slot_ids[None, :] == own_ids.reshape(-1)[:, None]).astype(jnp.bfloat16)
    buffer = jnp.dot(pick_own, image_rows, preferred_element_type=jnp.float32).astype(jnp.bfloat16)
    received = lax.all_to_all(
        buffer.reshape(requests, quarter, width), "req", split_axis=0, concat_axis=0, tiled=True
    )
    received = advance(0, received)
    arrived = gather_shares(received.reshape(requests * quarter, width))
    slot_blocks = got_slots.reshape(requests, groups, quarter)
    slots = jnp.concatenate(
        [
            lax.dynamic_index_in_dim(slot_blocks, group ^ r, 1, keepdims=False).reshape(-1)
            for r in range(groups)
        ]
    )
    place = slots[None, :] == jnp.arange(seq_len)[:, None]
    placed = jnp.dot(place.astype(jnp.bfloat16), arrived, preferred_element_type=jnp.float32)
    hit = jnp.any(place, axis=1, keepdims=True)
    embedded = jnp.where(hit, placed.astype(jnp.bfloat16), text)

    attn_in = rms_scale(embedded, attn_gain).astype(jnp.bfloat16)
    qkv = jnp.dot(attn_in, wqkv, preferred_element_type=jnp.float32).astype(jnp.bfloat16)
    local_heads = wqkv.shape[1] // (3 * HD)
    qkv = qkv.reshape(seq_len, local_heads, 3, HD)
    query, keys, values = (qkv[:, :, 0], qkv[:, :, 1], qkv[:, :, 2])
    share_rows = seq_len // groups
    piece = share_rows // CHUNKS

    def chunk_of(array, j):
        cut = array.reshape(groups, CHUNKS, piece, *array.shape[1:])[:, j]
        return cut.reshape(groups * piece, *array.shape[1:])

    row_ids = jnp.arange(seq_len)
    block_ids = group ^ jnp.arange(groups)
    query_rows = (block_ids[:, None] * share_rows + jnp.arange(share_rows)).reshape(-1)
    query_blocks = query.reshape(groups, share_rows, local_heads, HD)
    query = jnp.concatenate(
        [
            lax.dynamic_index_in_dim(query_blocks, group ^ r, 0, keepdims=False)
            for r in range(groups)
        ],
        axis=0,
    )
    sums = []
    for j in range(CHUNKS):
        rows = chunk_of(query_rows, j)
        scores = (
            jnp.einsum("qhd,khd->hqk", chunk_of(query, j), keys, preferred_element_type=jnp.float32)
            / jnp.float32(HD) ** 0.5
        )
        causal = row_ids[None, :] <= rows[:, None]
        scores = jnp.where(causal[None], scores, jnp.float32(-1e30))
        peak = jnp.max(scores, axis=-1, keepdims=True)
        weights = jnp.exp(scores - peak)
        probs = (weights / jnp.sum(weights, axis=-1, keepdims=True)).astype(jnp.bfloat16)
        context = jnp.einsum(
            "hqk,khd->qhd", probs, values, preferred_element_type=jnp.float32
        ).astype(jnp.bfloat16)
        context = context.reshape(groups * piece, local_heads * HD)
        attn_part = jnp.dot(context, wo, preferred_element_type=jnp.float32)
        attn_part = attn_part.astype(jnp.bfloat16)
        if j == 0:
            attn_part = advance(1, attn_part)
        sums.append(reduce_share(attn_part))
    own_embedded = lax.dynamic_slice_in_dim(embedded, group * share_rows, share_rows, 0)
    resids, inputs = [], []
    for j in range(CHUNKS):
        own = own_embedded[j * piece : (j + 1) * piece]
        resid = own.astype(jnp.float32) + narrow_sum(*sums[j]).astype(jnp.float32)
        if j == 0:
            resid = advance(2, resid)
            advance(3, None)
        resids.append(resid)
        mlp_in = rms_scale(resid, mlp_gain).astype(jnp.bfloat16)
        mlp_in = jnp.dot(mlp_in, column_map, preferred_element_type=jnp.float32)
        inputs.append(gather_shares(mlp_in.astype(jnp.bfloat16)))
    w_in_full, w_out_full = gathered(0), gathered(1)
    outs = []
    for j in range(CHUNKS):
        mlp_in = inputs[j]
        upward = jnp.dot(mlp_in, w_in_full, preferred_element_type=jnp.float32)
        active = jax.nn.gelu(upward, approximate=False).astype(jnp.bfloat16)
        mlp_part = lax.dot_general(
            active, w_out_full, (((1,), (1,)), ((), ())), preferred_element_type=jnp.float32
        )
        terms = jnp.concatenate(reduce_share(mlp_part.astype(jnp.bfloat16)), axis=0)
        terms = lax.dot_general(
            terms, column_map, (((1,), (1,)), ((), ())), preferred_element_type=jnp.float32
        )
        mlp_share = terms[:piece] + terms[piece:]
        result = resids[j] + mlp_share
        ids = group * share_rows + j * piece + jnp.arange(piece)
        outs.append(jnp.where((ids < lengths[0])[:, None], result, 0.0).astype(jnp.bfloat16))
    return jnp.concatenate(outs, axis=0)


def solution(mesh):
    return jax.shard_map(
        shards,
        mesh=mesh,
        in_specs=(
            P("req", "mlp", None),
            P(),
            P("mlp", None),
            P("req"),
            P("req"),
            P("req", None),
            P(),
            P(None, "mlp"),
            P("mlp", None),
            P(),
            P("req", "mlp"),
            P("mlp", "req"),
        ),
        out_specs=P(("req", "mlp"), None),
        check_vma=False,
    )
```
